128 devices in a mesh: ctx: 32 (over z_lo, y, x), head: 4 (over z_hi, core).
Axes of the slice: x: 4, y: 4, z: 4 (z_hi: 2, z_lo: 2; z = z_hi * 2 + z_lo), core: 2. Of those that a mesh axis runs over, the one named last changes fastest.
Arguments:
- main_query: bfloat16 [4096, 73728], P('ctx', 'head'), as said below
- latents: bfloat16 [2048, 576], P('ctx'), may hold values from -6 to 6, as said below
- idx_query: bfloat16 [4096, 8192], P('ctx'), as said below
- idx_weight: float32 [4096, 64], P('ctx'), may hold values from -9 to 9
- idx_keys: bfloat16 [2048, 128], P('ctx'), may hold values from -6 to 6, as said below
- kl_cotangent: float32 [4096], P('ctx'), may hold values from 4 to 64
- query_start: int32 [1], replicated, may hold values from 1024 to 2047
- key_start: int32 [1], replicated, may hold values from 0 to 1023
Outputs:
- grad_query: float32 [4096, 8192], P('ctx', 'head')
- grad_weight: float32 [4096, 64], P('ctx', 'head')
- grad_keys: float32 [2048, 128], P(('ctx', 'head'))
The draws below stay inside these ranges and needn't reach their ends.
Inputs may be any that keep to these rules, and one draw needn't show every extreme that they name: `latents`: saved latent keys of order one. `idx_keys`: indexer keys of order one. `main_query`: attention queries; a few rows may be large. `idx_query`: indexer queries; a few rows may be large.
All inputs are finite; a program needn't handle non-finite values.
Results may differ from the reference program's by a relative error of at most 0.02.
Values may be sent and summed in bfloat16 or wider, within the bound.
No kernel may reach another device: no remote copies, remote signals or barrier semaphores. Data moves between devices by JAX's collectives and lax.ppermute only.
A program may use at most 128 MiB of HBM per device.

```python
import math
import jax
import jax.numpy as jnp
from jax import lax

LATENT = 576
MAIN_HEADS = 128
IDX_HEADS = 64
IDX_DIM = 128
QUERY_DEV = 128
QUERIES = 4096
KEYS = 2048
N_CTX = 32


def slab_draw(key):
    key_latent = jax.random.fold_in(key, 71)
    key_index = jax.random.fold_in(key, 72)
    key_main = jax.random.fold_in(key, 73)
    key_query = jax.random.fold_in(key, 74)
    key_weight = jax.random.fold_in(key, 75)
    latent_table = jnp.clip(jax.random.normal(key_latent, (KEYS, LATENT), jnp.float32), -6.0, 6.0)
    index_table = jnp.clip(jax.random.normal(key_index, (KEYS, IDX_DIM), jnp.float32), -6.0, 6.0)
    main_table = jnp.clip(jax.random.normal(key_main, (QUERIES, MAIN_HEADS, LATENT), jnp.float32), -6.0, 6.0)
    query_table = jnp.clip(jax.random.normal(key_query, (QUERIES, IDX_HEADS, IDX_DIM), jnp.float32), -6.0, 6.0)
    weight_table = 0.5 * jnp.clip(jax.random.normal(key_weight, (QUERIES, IDX_HEADS), jnp.float32), -6.0, 6.0)
    return (latent_table, index_table, main_table.reshape(QUERIES, MAIN_HEADS * LATENT), query_table.reshape(QUERIES, IDX_HEADS * IDX_DIM), weight_table)


def draw_latents(key, part):
    return slab_draw(key)[0].astype(jnp.bfloat16)


def draw_idx_keys(key, part):
    return slab_draw(key)[1].astype(jnp.bfloat16)


def draw_main_query(key, part):
    return slab_draw(key)[2].astype(jnp.bfloat16)


def draw_idx_query(key, part):
    return slab_draw(key)[3].astype(jnp.bfloat16)


def draw_idx_weight(key, part):
    return slab_draw(key)[4]


def shard_levels(rng, shape, shards, smallest, top_value):
    loudness, own = 1.0, jax.random.fold_in(rng, 6)
    for position, shards_of in shards:
        heights = jnp.exp(jax.random.uniform(jax.random.fold_in(own, position), (shards_of,), jnp.float32, smallest / len(shards), top_value / len(shards)))
        loudness = loudness * jnp.repeat(heights, shape[position] // shards_of).reshape([-1 if axis == position else 1 for axis in range(len(shape))])
    return loudness


def setup_inputs(seed: int = 0) -> dict:
    streams_of = jax.random.split(jax.random.key(seed), 9)
    main_query = draw_main_query(jax.random.fold_in(streams_of[8], 71), 0)
    latents = draw_latents(jax.random.fold_in(streams_of[8], 71), 0)
    idx_query = draw_idx_query(jax.random.fold_in(streams_of[8], 71), 0)
    idx_weight = draw_idx_weight(jax.random.fold_in(streams_of[8], 71), 0)
    idx_keys = draw_idx_keys(jax.random.fold_in(streams_of[8], 71), 0)
    kl_cotangent = jnp.clip(jnp.exp(math.log(64.0) - 2.7725887 * jax.random.uniform(streams_of[5], (QUERIES,), jnp.float32) ** shard_levels(streams_of[5], (QUERIES,), ((0, 32),), -0.2, 0.2)), 4.0, 64.0)
    query_start = jax.random.randint(streams_of[6], (1,), KEYS // 2, KEYS).astype(jnp.int32)
    key_start = jax.random.randint(streams_of[7], (1,), 0, KEYS // 2).astype(jnp.int32)
    return dict(main_query=main_query, latents=latents, idx_query=idx_query, idx_weight=idx_weight, idx_keys=idx_keys, kl_cotangent=kl_cotangent, query_start=query_start, key_start=key_start)


NEGATIVE = -1e30
MAIN_SCALE = 192.0 ** -0.5


def masked_softmax(values, visible):
    values = jnp.where(visible, values, NEGATIVE)
    largest = jnp.max(values, axis=-1, keepdims=True)
    weights = jnp.where(visible, jnp.exp(values - largest), 0.0)
    return weights / jnp.sum(weights, axis=-1, keepdims=True)


def reference(main_query, latents, idx_query, idx_weight, idx_keys, kl_cotangent, query_start, key_start):
    queries_main = main_query.reshape(QUERIES, MAIN_HEADS, LATENT)
    queries_index = idx_query.reshape(QUERIES, IDX_HEADS, IDX_DIM)
    query_position = query_start[0] + jnp.arange(QUERIES, dtype=jnp.int32)
    key_position = key_start[0] + jnp.arange(KEYS, dtype=jnp.int32)
    scale = IDX_DIM ** -0.5

    def one_block(key_total, block_index):
        start = (block_index * QUERY_DEV).astype(jnp.int32)
        block_main = lax.dynamic_slice_in_dim(queries_main, start, QUERY_DEV, 0)
        block_index_q = lax.dynamic_slice_in_dim(queries_index, start, QUERY_DEV, 0)
        block_weight = lax.dynamic_slice_in_dim(idx_weight, start, QUERY_DEV, 0)
        block_cotangent = lax.dynamic_slice_in_dim(kl_cotangent, start, QUERY_DEV, 0)
        block_position = lax.dynamic_slice_in_dim(query_position, start, QUERY_DEV, 0)
        visible = key_position[None, :] <= block_position[:, None]

        def add_head(head_number, totals):
            head_query = lax.dynamic_index_in_dim(block_main, head_number, 1, keepdims=False)
            scores = jnp.dot(head_query, latents.T, preferred_element_type=jnp.float32) * MAIN_SCALE
            return totals + masked_softmax(scores, visible)

        totals = lax.fori_loop(0, MAIN_HEADS, add_head, jnp.zeros((QUERY_DEV, KEYS), jnp.float32))
        target = totals / MAIN_HEADS
        inner = jnp.einsum("bjd,kd->bjk", block_index_q.astype(jnp.float32), idx_keys.astype(jnp.float32)) * scale
        active = jnp.maximum(inner, 0.0)
        logits = jnp.sum(block_weight[:, :, None] * active, axis=1)
        chance = masked_softmax(logits, visible)
        upstream = block_cotangent[:, None] * (chance - target)
        grad_inner = jnp.where(inner > 0.0, upstream[:, None, :] * block_weight[:, :, None], 0.0).astype(jnp.bfloat16)
        weight_grad = jnp.sum(upstream[:, None, :] * active, axis=-1)
        query_grad = jnp.einsum("bjk,kd->bjd", grad_inner.astype(jnp.float32), idx_keys.astype(jnp.float32)) * scale
        key_grad = jnp.einsum("bjk,bjd->kd", grad_inner.astype(jnp.float32), block_index_q.astype(jnp.float32)) * scale
        return key_total + key_grad, (query_grad.reshape(QUERY_DEV, IDX_HEADS * IDX_DIM), weight_grad)

    key_total, (query_grads, weight_grads) = lax.scan(one_block, jnp.zeros((KEYS, IDX_DIM), jnp.float32), jnp.arange(N_CTX, dtype=jnp.int32))
    grad_query = query_grads.reshape(QUERIES, IDX_HEADS * IDX_DIM)
    grad_weight = weight_grads.reshape(QUERIES, IDX_HEADS)
    return grad_query, grad_weight, key_total
```

```python
import functools
import math

import jax
import jax.numpy as jnp
from jax import lax
from jax.experimental import pallas as pl
from jax.experimental.pallas import tpu as pltpu
from jax.sharding import Mesh
from jax.sharding import PartitionSpec as P

CTX = ("ctx_0", "ctx_1", "ctx_2")
HEAD = ("far", "core")
ALL = CTX + HEAD

MAIN_SCALE = 192.0 ** (-0.5)
LOG2E = math.log2(math.e)
bf16, f32 = jnp.bfloat16, jnp.float32


def key_of(place):
    return ((place >> 5) & 31) * 64 + (place >> 10) * 32 + (place & 31)


def lay_halves(keys, own, other, core, width):
    half = own.shape[0]
    keys[pl.ds(pl.multiple_of(core * half, half), half), 0:width] = own[...]
    keys[pl.ds(pl.multiple_of((1 - core) * half, half), half), 0:width] = other[...]


def head_kernel(where, q_ref, own_ref, other_ref, out_ref, keys, pair, scores, probs, acc):
    rows, width = q_ref.shape[0], own_ref.shape[1]
    n_keys = 2 * own_ref.shape[0]
    pairs = q_ref.shape[1] // (2 * width)
    wide = keys.shape[1] - rows
    lay_halves(keys, own_ref, other_ref, where[0], width)
    keys[:, width:wide] = jnp.zeros((n_keys, wide - width), bf16)
    place = lax.broadcasted_iota(jnp.int32, (n_keys, rows), 0)
    query = lax.broadcasted_iota(jnp.int32, (n_keys, rows), 1)
    keys[:, wide:] = jnp.where(key_of(place) > query + where[1], -1e30, 0.0).astype(bf16)
    pair[:, width:wide] = jnp.zeros((2 * rows, wide - width), bf16)
    row = lax.broadcasted_iota(jnp.int32, (2 * rows, rows), 0)
    lane = lax.broadcasted_iota(jnp.int32, (2 * rows, rows), 1)
    pair[:, wide:] = jnp.where((row & (rows - 1)) == lane, 1.0, 0.0).astype(bf16)
    acc[...] = jnp.zeros(acc.shape, f32)
    scale = MAIN_SCALE * LOG2E
    vec = (8, 2 * rows)
    tall = (n_keys // 8, 8, 2 * rows)

    def step(p, product, exponent, add, shift, recip):
        top = total = jnp.zeros(vec, f32)
        if product:
            both = q_ref[:, pl.ds(pl.multiple_of(p * (2 * width), 128), 2 * width)]
            pair[0:rows, 0:width] = both[:, :width]
            pair[rows:, 0:width] = both[:, width:]
        if add:
            old = (probs[...].astype(f32).reshape(tall) * recip[None]).reshape(n_keys, 2 * rows)
            acc[...] += old[:, :rows] + old[:, rows:]
        if exponent:
            e = jnp.exp2(scores[...].reshape(tall) * scale - shift[None])
            total = jnp.sum(e, axis=0)
            probs[...] = e.reshape(n_keys, 2 * rows).astype(bf16)
        if product:
            new = lax.dot_general(
                keys[...], pair[...], (((1,), (1,)), ((), ())), preferred_element_type=f32
            )
            scores[...] = new
            top = jnp.max(new.reshape(tall), axis=0)
        top = jnp.broadcast_to(jnp.max(top, axis=0, keepdims=True), vec)
        total = jnp.broadcast_to(jnp.sum(total, axis=0, keepdims=True), vec)
        return top * scale, 1.0 / jnp.maximum(total, 1e-30)

    zero = jnp.zeros(vec, f32)
    shift, _ = step(0, True, False, False, zero, zero)
    shift, recip = step(1, True, True, False, shift, zero)
    shift, recip = lax.fori_loop(
        2, pairs, lambda p, c: step(p, True, True, True, *c), (shift, recip)
    )
    _, recip = step(pairs, False, True, True, shift, recip)
    step(pairs, False, False, True, zero, recip)
    out_ref[...] = (acc[...] * where[2]).T.astype(bf16)


def head_totals(where, q, own, other):
    rows = q.shape[0]
    n_keys = 2 * own.shape[0]
    vmem = pl.BlockSpec(memory_space=pltpu.VMEM)

    def body(where, *refs):
        head_kernel((where[0], where[1], jnp.float32(1.0 / 128.0)), *refs)

    return pl.pallas_call(
        body,
        out_shape=jax.ShapeDtypeStruct((rows, n_keys), bf16),
        in_specs=[pl.BlockSpec(memory_space=pltpu.SMEM), vmem, vmem, vmem],
        out_specs=vmem,
        scratch_shapes=[
            pltpu.VMEM((n_keys, 768), bf16),
            pltpu.VMEM((2 * rows, 768), bf16),
            pltpu.VMEM((n_keys, 2 * rows), f32),
            pltpu.VMEM((n_keys, 2 * rows), bf16),
            pltpu.VMEM((n_keys, rows), f32),
        ],
        compiler_params=pltpu.CompilerParams(vmem_limit_bytes=56 * 2**20),
        cost_estimate=pl.CostEstimate(
            flops=2 * 32 * rows * n_keys * 768, bytes_accessed=8 * 2**20, transcendentals=2**23
        ),
        name="head_totals",
    )(where, q, own, other)


IDX_GROUP = 8


def forward_kernel(where, q_ref, w_ref, own_ref, other_ref, kl_ref, mask_ref, chance_ref, keys, block, logits):
    g = pl.program_id(0)
    rows, dim = q_ref.shape[0], keys.shape[1]

    @pl.when(g == 0)
    def _():
        lay_halves(keys, own_ref, other_ref, where[0], dim)
        logits[...] = jnp.zeros(logits.shape, f32)

    for j in range(IDX_GROUP):
        block[j * rows : (j + 1) * rows, :] = q_ref[:, j * dim : (j + 1) * dim]
    inner = lax.dot_general(
        block[...], keys[...], (((1,), (1,)), ((), ())), preferred_element_type=f32
    )
    mask_ref[...] = jnp.where(inner > 0.0, 1.0, 0.0).astype(bf16)
    active = jnp.maximum(inner, 0.0)
    weights = w_ref[0] * (dim ** (-0.5))
    total = logits[...]
    for j in range(IDX_GROUP):
        total += active[j * rows : (j + 1) * rows] * weights[:, j : j + 1]
    logits[...] = total

    @pl.when(g == pl.num_programs(0) - 1)
    def _():
        place = lax.broadcasted_iota(jnp.int32, logits.shape, 1)
        query = lax.broadcasted_iota(jnp.int32, logits.shape, 0) + where[2] * rows
        seen = key_of(place) <= query + where[1]
        values = jnp.where(seen, total, -1e30)
        e = jnp.where(seen, jnp.exp(values - jnp.max(values, axis=1, keepdims=True)), 0.0)
        chance_ref[...] = e * (kl_ref[...] / jnp.sum(e, axis=1, keepdims=True))


def index_forward(where, q, w, own, other, kl):
    rows, dim = kl.shape[0], own.shape[1]
    n_keys = 2 * own.shape[0]
    heads = q.shape[1] // dim
    wide = IDX_GROUP * dim
    return pl.pallas_call(
        forward_kernel,
        grid_spec=pltpu.PrefetchScalarGridSpec(
            num_scalar_prefetch=1,
            grid=(heads // IDX_GROUP,),
            in_specs=[
                pl.BlockSpec((rows, wide), lambda g, where: (where[2], g)),
                pl.BlockSpec((1, rows, IDX_GROUP), lambda g, where: (g, 0, 0)),
                pl.BlockSpec((n_keys // 2, dim), lambda g, where: (0, 0)),
                pl.BlockSpec((n_keys // 2, dim), lambda g, where: (0, 0)),
                pl.BlockSpec((rows, 1), lambda g, where: (0, 0)),
            ],
            out_specs=[
                pl.BlockSpec((IDX_GROUP * rows, n_keys), lambda g, where: (g, 0)),
                pl.BlockSpec((rows, n_keys), lambda g, where: (0, 0)),
            ],
            scratch_shapes=[
                pltpu.VMEM((n_keys, dim), bf16),
                pltpu.VMEM((IDX_GROUP * rows, dim), bf16),
                pltpu.VMEM((rows, n_keys), f32),
            ],
        ),
        out_shape=[
            jax.ShapeDtypeStruct((heads * rows, n_keys), bf16),
            jax.ShapeDtypeStruct((rows, n_keys), f32),
        ],
        compiler_params=pltpu.CompilerParams(vmem_limit_bytes=40 * 2**20),
        cost_estimate=pl.CostEstimate(
            flops=2 * heads * rows * n_keys * 256, bytes_accessed=10 * 2**20, transcendentals=2**16
        ),
        name="index_forward",
    )(where, q, w, own, other, kl)


def backward_kernel(where, parts_ref, chance_ref, kl_ref, mask_ref, q_ref, w_ref, own_ref, other_ref, grad_ref, gk_ref, keys, upstream, block, acc):
    g = pl.program_id(0)
    rows, dim = q_ref.shape[0], keys.shape[1]
    scale = dim ** (-0.5)

    @pl.when(g == 0)
    def _():
        lay_halves(keys, own_ref, other_ref, where[0], dim)
        target = parts_ref[0].astype(f32)
        for h in range(1, parts_ref.shape[0]):
            target += parts_ref[h].astype(f32)
        upstream[...] = (chance_ref[...] - kl_ref[...] * target).astype(bf16)
        acc[...] = jnp.zeros(acc.shape, f32)
        grad_ref[:, :, 2048:] = jnp.zeros((4, rows, 128), bf16)

    up = upstream[...]
    masked = mask_ref[...] * jnp.concatenate([up] * IDX_GROUP, axis=0)
    plain = (
        lax.dot_general(masked, keys[...], (((1,), (0,)), ((), ())), preferred_element_type=f32)
        * scale
    )
    owner, side = g // 2, g % 2
    lane = lax.broadcasted_iota(jnp.int32, (rows, 128), 1)
    sums = jnp.zeros((rows, 128), f32)
    for j in range(IDX_GROUP):
        q = q_ref[:, j * dim : (j + 1) * dim].astype(f32)
        gain = w_ref[0, :, j : j + 1]
        own = plain[j * rows : (j + 1) * rows]
        block[j * rows : (j + 1) * rows, :] = (q * gain).astype(bf16)
        grad_ref[owner, :, pl.ds(pl.multiple_of(side * (IDX_GROUP * dim) + j * dim, dim), dim)] = (
            own * gain
        ).astype(bf16)
        sums = jnp.where(
            lane == side * IDX_GROUP + j, jnp.sum(q * own, axis=1, keepdims=True), sums
        )
    grad_ref[owner, :, 2048:] += sums.astype(bf16)
    acc[...] += lax.dot_general(
        block[...], masked, (((0,), (0,)), ((), ())), preferred_element_type=f32
    )

    @pl.when(g == pl.num_programs(0) - 1)
    def _():
        n_keys = acc.shape[1]
        for t in range(n_keys // 128):
            piece = (acc[:, t * 128 : (t + 1) * 128] * scale).T.astype(bf16)
            for b in range(4):
                place = t * 128 + b * 32
                key = ((place >> 5) & 31) * 64 + (place >> 10) * 32
                gk_ref[key : key + 32, :] = piece[b * 32 : (b + 1) * 32]


def index_backward(where, parts, chance, kl, mask, q, w, own, other):
    rows, dim = kl.shape[0], own.shape[1]
    n_keys = 2 * own.shape[0]
    heads = q.shape[1] // dim
    wide = IDX_GROUP * dim

    def whole(*shape):
        return pl.BlockSpec(shape, lambda g, where: (0,) * len(shape))

    return pl.pallas_call(
        backward_kernel,
        grid_spec=pltpu.PrefetchScalarGridSpec(
            num_scalar_prefetch=1,
            grid=(heads // IDX_GROUP,),
            in_specs=[
                whole(4, rows, n_keys),
                whole(rows, n_keys),
                whole(rows, 1),
                pl.BlockSpec((IDX_GROUP * rows, n_keys), lambda g, where: (g, 0)),
                pl.BlockSpec((rows, wide), lambda g, where: (where[2], g)),
                pl.BlockSpec((1, rows, IDX_GROUP), lambda g, where: (g, 0, 0)),
                whole(n_keys // 2, dim),
                whole(n_keys // 2, dim),
            ],
            out_specs=[whole(4, rows, 2048 + 128), whole(n_keys, dim)],
            scratch_shapes=[
                pltpu.VMEM((n_keys, dim), bf16),
                pltpu.VMEM((rows, n_keys), bf16),
                pltpu.VMEM((IDX_GROUP * rows, dim), bf16),
                pltpu.VMEM((dim, n_keys), f32),
            ],
        ),
        out_shape=[
            jax.ShapeDtypeStruct((4, rows, 2048 + 128), bf16),
            jax.ShapeDtypeStruct((n_keys, dim), bf16),
        ],
        compiler_params=pltpu.CompilerParams(vmem_limit_bytes=40 * 2**20),
        cost_estimate=pl.CostEstimate(
            flops=8 * heads * rows * n_keys * 128, bytes_accessed=10 * 2**20, transcendentals=0
        ),
        name="index_backward",
    )(where, parts, chance, kl, mask, q, w, own, other)


def to_all(piece, axes):
    copies = jnp.broadcast_to(piece, (lax.axis_size(axes), *piece.shape))
    return lax.all_to_all(copies, axes, split_axis=0, concat_axis=0, tiled=True)


def gather_halves(array, core):
    half = array.shape[0] // 2
    mine = to_all(lax.dynamic_slice_in_dim(array, core * half, half, 0), CTX)
    mine = mine.reshape(-1, array.shape[1])
    return mine, lax.ppermute(mine, "core", [(0, 1), (1, 0)])


def shards(
    main_query, latents, idx_query, idx_weight, idx_keys, kl_cotangent, query_start, key_start
):
    rows = main_query.shape[0]
    core = lax.axis_index("core")
    head = lax.axis_index(HEAD)
    heads = lax.axis_size(HEAD)
    few = rows // heads
    offset = query_start[0] + lax.axis_index(CTX) * rows - key_start[0]
    where = jnp.stack([core, offset, head]).astype(jnp.int32)

    own_index, other_index = gather_halves(idx_keys, core)
    latents, _ = lax.optimization_barrier((latents, own_index))
    own, other = gather_halves(latents, core)

    kl = lax.dynamic_slice_in_dim(kl_cotangent, head * few, few, 0)[:, None]
    w = lax.dynamic_slice_in_dim(idx_weight, head * few, few, 0)
    w = w.reshape(few, -1, IDX_GROUP).transpose(1, 0, 2)
    mask, chance = index_forward(where, idx_query, w, own_index, other_index, kl)

    target = head_totals(where, main_query, own, other)
    parts = lax.all_to_all(target.reshape(heads, few, -1), HEAD, 0, 0, tiled=True)
    grad, gk = index_backward(
        where, parts, chance, kl, mask, idx_query, w, own_index, other_index
    )
    pieces = lax.all_to_all(gk.reshape(lax.axis_size(ALL), -1, gk.shape[1]), ALL, 0, 0, tiled=True)
    grad_keys = jnp.sum(pieces.astype(f32), axis=0)
    grad = lax.all_to_all(grad, HEAD, 0, 0, tiled=True).reshape(rows, -1).astype(f32)
    return grad[:, :2048], grad[:, 2048 : 2048 + 16], grad_keys


def solution(mesh):
    torus = Mesh(mesh.devices.reshape(2, 4, 4, 2, 2), ALL)
    placed = (
        P(CTX, HEAD),
        P(CTX, None),
        P(CTX, None),
        P(CTX, None),
        P(CTX, None),
        P(CTX),
        P(),
        P(),
    )
    return jax.shard_map(
        shards,
        mesh=torus,
        in_specs=placed,
        out_specs=(P(CTX, HEAD), P(CTX, HEAD), P(ALL, None)),
        check_vma=False,
    )
```

```python
import math

import jax
import jax.numpy as jnp
from jax import lax
from jax.experimental import pallas as pl
from jax.experimental.pallas import tpu as pltpu
from jax.sharding import Mesh
from jax.sharding import PartitionSpec as P

CTX = ("ctx_0", "ctx_1", "ctx_2")
HEAD = ("far", "core")
ALL = CTX + HEAD

LATENT = 576
MAIN_SCALE = 192.0 ** (-0.5)
LOG2E = math.log2(math.e)
bf16, f32 = jnp.bfloat16, jnp.float32

SIDES = 2


def key_of(place):
    half, side, ctx = place >> 10, (place >> 9) & 1, (place >> 4) & 31
    return ctx * 64 + half * 32 + side * 16 + (place & 15)


def lay_index_keys(keys, pieces, core):
    count = pieces[0].shape[0]
    for n, piece in enumerate(pieces):
        spot = ((core ^ (n // SIDES)) * SIDES + n % SIDES) * count
        keys[pl.ds(pl.multiple_of(spot, count), count), :] = piece[...]


def index_key_specs(own):
    first = own.shape[1] // IDX_DIM - SIDES
    return [
        pl.BlockSpec((own.shape[0], IDX_DIM), lambda g, where, at=first + side: (0, at))
        for _ in range(2)
        for side in range(SIDES)
    ]


def head_kernel(where, q_hbm, own_hbm, other_hbm, *refs):
    outs, (keys, queries, pair, scores, probs, acc, turned, sems) = refs[:4], refs[4:]
    pairs, rows, both_width = queries.shape
    width = both_width // 2
    count = own_hbm.shape[0]
    n_keys = 2 * SIDES * count
    wide = keys.shape[1] - rows
    body = wide - rows

    def key_copies(k, source):
        for side in range(SIDES):
            spot = ((where[0] ^ k) * SIDES + side) * count
            at = pl.ds(pl.multiple_of(spot, count), count)
            sem = (k * SIDES + side) * 2
            yield pltpu.make_async_copy(
                source.at[:, pl.ds(side * body, body)], keys.at[at, pl.ds(0, body)], sems.at[sem]
            )
            yield pltpu.make_async_copy(
                source.at[:, pl.ds(SIDES * body, rows)],
                keys.at[at, pl.ds(body, rows)],
                sems.at[sem + 1],
            )

    def query_copy(p):
        at = pl.multiple_of(p * both_width, 128)
        return pltpu.make_async_copy(
            q_hbm.at[:, pl.ds(at, both_width)], queries.at[p], sems.at[8 + p]
        )

    for k, source in enumerate((own_hbm, other_hbm)):
        for copy in key_copies(k, source):
            copy.start()
    query_copy(0).start()
    for p in range(1, pairs):
        query_copy(p).start()
    place = lax.broadcasted_iota(jnp.int32, (n_keys, rows), 0)
    query = lax.broadcasted_iota(jnp.int32, (n_keys, rows), 1)
    keys[:, wide:] = jnp.where(key_of(place) > query + where[1], -1e30, 0.0).astype(bf16)
    row = lax.broadcasted_iota(jnp.int32, (2 * rows, rows), 0)
    lane = lax.broadcasted_iota(jnp.int32, (2 * rows, rows), 1)
    pair[:, wide:] = jnp.where((row & (rows - 1)) == lane, 1.0, 0.0).astype(bf16)
    acc[...] = jnp.zeros(acc.shape, f32)
    scale = MAIN_SCALE * LOG2E
    vec = (8, 2 * rows)
    tall = (n_keys // 8, 8, 2 * rows)
    for k, source in enumerate((own_hbm, other_hbm)):
        for copy in key_copies(k, source):
            copy.wait()
    lane = lax.broadcasted_iota(jnp.int32, (count, rows), 1)
    for n in range(2 * SIDES):
        at = slice(n * count, (n + 1) * count)
        rest = keys[at, body:wide].astype(f32)
        keys[at, body:wide] = jnp.where(lane // (wide - width) == n % SIDES, rest, 0.0).astype(bf16)

    def add_pair(recip):
        old = (probs[...].astype(f32).reshape(tall) * recip[None]).reshape(n_keys, 2 * rows)
        acc[...] += old[:, :rows] + old[:, rows:]

    def step(p, carry):
        shift, recip = carry
        last = jnp.minimum(p, pairs - 1)

        @pl.when(p < pairs)
        def _():
            query_copy(p).wait()

        both = queries[last]
        for h in range(2):
            at = slice(h * rows, (h + 1) * rows)
            pair[at, 0:width] = both[:, h * width : (h + 1) * width]
            pair[at, width:wide] = both[:, h * width + body : (h + 1) * width]
        add_pair(recip)
        e = jnp.exp2(scores[...].reshape(tall) * scale - shift[None])
        total = jnp.sum(e, axis=0)
        probs[...] = e.reshape(n_keys, 2 * rows).astype(bf16)
        new = lax.dot_general(
            keys[...], pair[...], (((1,), (1,)), ((), ())), preferred_element_type=f32
        )
        scores[...] = new
        top = jnp.max(new.reshape(tall), axis=0)
        top = jnp.broadcast_to(jnp.max(top, axis=0, keepdims=True), vec)
        total = jnp.broadcast_to(jnp.sum(total, axis=0, keepdims=True), vec)
        return top * scale, jnp.where(p > 0, 1.0 / total, 0.0)

    scores[...] = jnp.zeros(scores.shape, f32)
    probs[...] = jnp.zeros(probs.shape, bf16)
    zero = jnp.zeros(vec, f32)
    _, recip = lax.fori_loop(0, pairs + 1, step, (zero, zero))
    add_pair(recip)
    turned[...] = (acc[...] * (1.0 / 128.0)).T.astype(bf16)
    few = rows // 4
    for k in range(4):
        outs[k][...] = turned[pl.ds(pl.multiple_of((where[2] ^ k) * few, few), few), :]


def head_totals(where, q, own, other):
    rows, columns = q.shape
    n_keys = 2 * SIDES * own.shape[0]
    pairs = columns // (2 * LATENT)
    vmem = pl.BlockSpec(memory_space=pltpu.VMEM)
    anywhere = pl.BlockSpec(memory_space=pl.ANY)
    return pl.pallas_call(
        head_kernel,
        out_shape=[jax.ShapeDtypeStruct((rows // 4, n_keys), bf16)] * 4,
        in_specs=[
            pl.BlockSpec(memory_space=pltpu.SMEM),
            pl.BlockSpec(memory_space=pltpu.HBM),
            anywhere,
            anywhere,
        ],
        out_specs=[vmem] * 4,
        scratch_shapes=[
            pltpu.VMEM((n_keys, 768), bf16),
            pltpu.VMEM((pairs, rows, 2 * LATENT), bf16),
            pltpu.VMEM((2 * rows, 768), bf16),
            pltpu.VMEM((n_keys, 2 * rows), f32),
            pltpu.VMEM((n_keys, 2 * rows), bf16),
            pltpu.VMEM((n_keys, rows), f32),
            pltpu.VMEM((rows, n_keys), bf16),
            pltpu.SemaphoreType.DMA((8 + pairs,)),
        ],
        compiler_params=pltpu.CompilerParams(vmem_limit_bytes=56 * 2**20),
        cost_estimate=pl.CostEstimate(
            flops=2 * 32 * rows * n_keys * 768, bytes_accessed=8 * 2**20, transcendentals=2**23
        ),
        name="head_totals",
    )(where, q, own, other)


IDX_GROUP = 32
IDX_DIM = 128
OWN_HEADS = 16
BIT = [1 << j for j in range(31)] + [-(2**31)]


def forward_kernel(where, q_ref, w_ref, *refs):
    pieces, (kl_ref, bits_ref, chance_ref, keys, block, logits) = refs[:4], refs[4:]
    g = pl.program_id(0)
    rows, dim = q_ref.shape[0], keys.shape[1]

    @pl.when(g == 0)
    def _():
        lay_index_keys(keys, pieces, where[0])
        logits[...] = jnp.zeros(logits.shape, f32)

    for j in range(IDX_GROUP):
        block[j * rows : (j + 1) * rows, :] = q_ref[:, j * dim : (j + 1) * dim]
    inner = lax.dot_general(
        block[...], keys[...], (((1,), (1,)), ((), ())), preferred_element_type=f32
    )
    weights = w_ref[0] * (dim ** (-0.5))
    total = logits[...]
    bits = jnp.zeros(total.shape, jnp.int32)
    for j in range(IDX_GROUP):
        part = inner[j * rows : (j + 1) * rows]
        total += jnp.maximum(part, 0.0) * weights[:, j : j + 1]
        bits = bits | jnp.where(part > 0.0, BIT[j], 0)
    logits[...] = total
    bits_ref[...] = bits

    @pl.when(g == pl.num_programs(0) - 1)
    def _():
        place = lax.broadcasted_iota(jnp.int32, logits.shape, 1)
        query = lax.broadcasted_iota(jnp.int32, logits.shape, 0) + where[2] * rows
        seen = key_of(place) <= query + where[1]
        values = jnp.where(seen, total, -1e30)
        e = jnp.where(seen, jnp.exp(values - jnp.max(values, axis=1, keepdims=True)), 0.0)
        chance_ref[...] = e * (kl_ref[...] / jnp.sum(e, axis=1, keepdims=True))


def index_forward(where, q, w, own, other, kl):
    rows, dim = kl.shape[0], IDX_DIM
    n_keys = 2 * SIDES * own.shape[0]
    heads = q.shape[1] // dim
    wide = IDX_GROUP * dim
    return pl.pallas_call(
        forward_kernel,
        grid_spec=pltpu.PrefetchScalarGridSpec(
            num_scalar_prefetch=1,
            grid=(heads // IDX_GROUP,),
            in_specs=[
                pl.BlockSpec((rows, wide), lambda g, where: (0, g)),
                pl.BlockSpec((1, rows, IDX_GROUP), lambda g, where: (g, 0, 0)),
                *index_key_specs(own),
                pl.BlockSpec((rows, 1), lambda g, where: (0, 0)),
            ],
            out_specs=[
                pl.BlockSpec((rows, n_keys), lambda g, where: (g, 0)),
                pl.BlockSpec((rows, n_keys), lambda g, where: (0, 0)),
            ],
            scratch_shapes=[
                pltpu.VMEM((n_keys, dim), bf16),
                pltpu.VMEM((IDX_GROUP * rows, dim), bf16),
                pltpu.VMEM((rows, n_keys), f32),
            ],
        ),
        out_shape=[
            jax.ShapeDtypeStruct((heads // IDX_GROUP * rows, n_keys), jnp.int32),
            jax.ShapeDtypeStruct((rows, n_keys), f32),
        ],
        compiler_params=pltpu.CompilerParams(vmem_limit_bytes=24 * 2**20),
        cost_estimate=pl.CostEstimate(
            flops=2 * heads * rows * n_keys * 256, bytes_accessed=10 * 2**20, transcendentals=2**16
        ),
        name="index_forward",
    )(where, q, w, own, own, other, other, kl)


def lay_masked(bits_ref, upstream, masked):
    rows = bits_ref.shape[0]
    bits, up = bits_ref[...], upstream[...]
    for j in range(IDX_GROUP):
        masked[j * rows : (j + 1) * rows, :] = jnp.where(bits & BIT[j] != 0, up, 0.0).astype(bf16)


def query_kernel(where, upstream_ref, bits_ref, q_ref, w_ref, *refs):
    pieces, outs, (keys, masked, grad_ref) = refs[:4], refs[4:8], refs[8:]
    g = pl.program_id(0)
    rows, dim = q_ref.shape[0], keys.shape[1]
    wide = grad_ref.shape[2] - 128

    @pl.when(g == 0)
    def _():
        lay_index_keys(keys, pieces, where[0])

    lay_masked(bits_ref, upstream_ref, masked)
    plain = lax.dot_general(
        masked[...], keys[...], (((1,), (0,)), ((), ())), preferred_element_type=f32
    ) * (dim ** (-0.5))
    lane = lax.broadcasted_iota(jnp.int32, (rows, 128), 1)
    for first in range(0, IDX_GROUP, OWN_HEADS):
        owner = g * (IDX_GROUP // OWN_HEADS) + first // OWN_HEADS
        sums = jnp.zeros((rows, 128), f32)
        for n in range(OWN_HEADS):
            j = first + n
            q = q_ref[:, j * dim : (j + 1) * dim].astype(f32)
            part = plain[j * rows : (j + 1) * rows]
            gain = w_ref[0, :, j : j + 1]
            grad_ref[owner, :, n * dim : (n + 1) * dim] = (part * gain).astype(bf16)
            sums = jnp.where(lane == n, jnp.sum(q * part, axis=1, keepdims=True), sums)
        grad_ref[owner, :, wide:] = sums.astype(bf16)

    @pl.when(g == pl.num_programs(0) - 1)
    def _():
        for k in range(4):
            outs[k][...] = grad_ref[where[2] ^ k]


def key_kernel(where, *refs):
    parts, refs = refs[:4], refs[4:]
    chance_ref, kl_ref, bits_ref, q_ref, w_ref, gk_ref, upstream_ref, masked, block, acc = refs
    g = pl.program_id(0)
    rows, dim = q_ref.shape[0], block.shape[1]

    @pl.when(g == 0)
    def _():
        target = parts[0][...].astype(f32)
        for k in range(1, 4):
            target += parts[k][...].astype(f32)
        upstream_ref[...] = chance_ref[...] - kl_ref[...] * target
        acc[...] = jnp.zeros(acc.shape, f32)

    lay_masked(bits_ref, upstream_ref, masked)
    for j in range(IDX_GROUP):
        q = q_ref[:, j * dim : (j + 1) * dim].astype(f32)
        block[j * rows : (j + 1) * rows, :] = (q * w_ref[0, :, j : j + 1]).astype(bf16)
    acc[...] += lax.dot_general(
        block[...], masked[...], (((0,), (0,)), ((), ())), preferred_element_type=f32
    )

    @pl.when(g == pl.num_programs(0) - 1)
    def _():
        for t in range(acc.shape[1] // 128):
            piece = (acc[:, t * 128 : (t + 1) * 128] * (dim ** (-0.5))).T.astype(bf16)
            for b in range(0, 128, 16):
                key = key_of(t * 128 + b)
                gk_ref[key : key + 16, :] = piece[b : b + 16]


def whole(*shape):
    return pl.BlockSpec(shape, lambda g, where: (0,) * len(shape))


def index_query_grads(where, upstream, bits, q, w, own, other):
    rows, n_keys = upstream.shape
    dim = IDX_DIM
    heads = q.shape[1] // dim
    out = jax.ShapeDtypeStruct((rows, heads // 4 * dim + 128), bf16)
    return pl.pallas_call(
        query_kernel,
        grid_spec=pltpu.PrefetchScalarGridSpec(
            num_scalar_prefetch=1,
            grid=(heads // IDX_GROUP,),
            in_specs=[
                whole(rows, n_keys),
                pl.BlockSpec((rows, n_keys), lambda g, where: (g, 0)),
                pl.BlockSpec((rows, IDX_GROUP * dim), lambda g, where: (0, g)),
                pl.BlockSpec((1, rows, IDX_GROUP), lambda g, where: (g, 0, 0)),
                *index_key_specs(own),
            ],
            out_specs=[whole(*out.shape)] * 4,
            scratch_shapes=[
                pltpu.VMEM((n_keys, dim), bf16),
                pltpu.VMEM((IDX_GROUP * rows, n_keys), bf16),
                pltpu.VMEM((4, *out.shape), bf16),
            ],
        ),
        out_shape=[out] * 4,
        compiler_params=pltpu.CompilerParams(vmem_limit_bytes=24 * 2**20),
        cost_estimate=pl.CostEstimate(
            flops=4 * heads * rows * n_keys * 128, bytes_accessed=6 * 2**20, transcendentals=0
        ),
        name="index_query_grads",
    )(where, upstream, bits, q, w, own, own, other, other)


def index_key_grads(where, parts, chance, kl, bits, q, w):
    rows, n_keys = chance.shape
    dim = IDX_DIM
    heads = q.shape[1] // dim
    return pl.pallas_call(
        key_kernel,
        grid_spec=pltpu.PrefetchScalarGridSpec(
            num_scalar_prefetch=1,
            grid=(heads // IDX_GROUP,),
            in_specs=[
                *[whole(rows, n_keys)] * 5,
                whole(rows, 1),
                pl.BlockSpec((rows, n_keys), lambda g, where: (g, 0)),
                pl.BlockSpec((rows, IDX_GROUP * dim), lambda g, where: (0, g)),
                pl.BlockSpec((1, rows, IDX_GROUP), lambda g, where: (g, 0, 0)),
            ],
            out_specs=[whole(n_keys, dim), whole(rows, n_keys)],
            scratch_shapes=[
                pltpu.VMEM((IDX_GROUP * rows, n_keys), bf16),
                pltpu.VMEM((IDX_GROUP * rows, dim), bf16),
                pltpu.VMEM((dim, n_keys), f32),
            ],
        ),
        out_shape=[
            jax.ShapeDtypeStruct((n_keys, dim), bf16),
            jax.ShapeDtypeStruct((rows, n_keys), f32),
        ],
        compiler_params=pltpu.CompilerParams(vmem_limit_bytes=24 * 2**20),
        cost_estimate=pl.CostEstimate(
            flops=4 * heads * rows * n_keys * 128, bytes_accessed=6 * 2**20, transcendentals=0
        ),
        name="index_key_grads",
    )(where, *parts, chance, kl, bits, q, w)


def to_all(piece, axes):
    copies = jnp.broadcast_to(piece, (lax.axis_size(axes), *piece.shape))
    return lax.all_to_all(copies, axes, split_axis=0, concat_axis=0, tiled=True)


def finish_kernel(where, *refs):
    grads, (key_ref, query_out, weight_out, key_out, wide_weight) = refs[:4], refs[4:]
    few, wide = grads[0].shape[0], query_out.shape[1]
    for k in range(4):
        at = pl.ds(pl.multiple_of((where[2] ^ k) * few, few), few)
        query_out[at, :] = grads[k][:, :wide].astype(f32)
        wide_weight[at, :] = grads[k][:, wide:].astype(f32)
    weight_out[...] = wide_weight[...].T[: weight_out.shape[0]]
    key_out[...] = jnp.sum(key_ref[...].astype(f32), axis=0)


def finish(where, grads, keys):
    rows = 4 * grads[0].shape[0]
    vmem = pl.BlockSpec(memory_space=pltpu.VMEM)
    return pl.pallas_call(
        finish_kernel,
        out_shape=[
            jax.ShapeDtypeStruct((rows, OWN_HEADS * IDX_DIM), f32),
            jax.ShapeDtypeStruct((OWN_HEADS, rows), f32),
            jax.ShapeDtypeStruct(keys.shape[1:], f32),
        ],
        in_specs=[pl.BlockSpec(memory_space=pltpu.SMEM)] + [vmem] * 5,
        out_specs=[vmem] * 3,
        scratch_shapes=[pltpu.VMEM((rows, 128), f32)],
        compiler_params=pltpu.CompilerParams(vmem_limit_bytes=16 * 2**20),
        cost_estimate=pl.CostEstimate(flops=2**20, bytes_accessed=2**21, transcendentals=0),
        name="finish",
    )(where, *grads, keys)


def swap_heads(pieces):
    count = len(pieces)
    return [pieces[0]] + [
        lax.ppermute(pieces[k], HEAD, [(h, h ^ k) for h in range(count)]) for k in range(1, count)
    ]


def shards(
    main_query, latents, idx_query, idx_weight, idx_keys, kl_cotangent, query_start, key_start
):
    rows = main_query.shape[0]
    core = lax.axis_index("core")
    head = lax.axis_index(HEAD)
    few = rows // lax.axis_size(HEAD)
    offset = query_start[0] + lax.axis_index(CTX) * rows - key_start[0]
    where = jnp.stack([core, offset, head]).astype(jnp.int32)

    half, side = latents.shape[0] // 2, latents.shape[0] // 4
    body = latents.shape[1] // 128 * 128
    lat = lax.dynamic_slice_in_dim(latents, core * half, half, 0)
    idx = lax.dynamic_slice_in_dim(idx_keys, core * half, half, 0)
    parts = [lat[:, :body], lat[:, body:], idx]
    slab = jnp.concatenate([p[at : at + side] for p in parts for at in (0, side)], axis=1)
    own = to_all(slab, CTX).reshape(-1, slab.shape[1])
    other = lax.ppermute(own, "core", [(0, 1), (1, 0)])

    kl = lax.dynamic_slice_in_dim(kl_cotangent, head * few, few, 0)[:, None]
    w = lax.dynamic_slice_in_dim(idx_weight, head * few, few, 0)
    w = w.reshape(few, -1, IDX_GROUP).transpose(1, 0, 2)

    few_queries = lax.dynamic_slice_in_dim(idx_query, head * few, few, 0)

    parts = swap_heads(head_totals(where, main_query, own, other))
    bits, chance = index_forward(where, few_queries, w, own, other, kl)
    gk, upstream = index_key_grads(where, parts, chance, kl, bits, few_queries, w)
    pieces = lax.all_to_all(gk.reshape(lax.axis_size(ALL), -1, gk.shape[1]), ALL, 0, 0, tiled=True)
    grads = index_query_grads(where, upstream, bits, few_queries, w, own, other)
    grad_query, grad_weight, grad_keys = finish(where, swap_heads(grads), pieces)
    return grad_query, grad_weight.T, grad_keys


def solution(mesh):
    torus = Mesh(mesh.devices.reshape(2, 4, 4, 2, 2), ALL)
    placed = (
        P(CTX, HEAD),
        P(CTX, None),
        P(CTX, None),
        P(CTX, None),
        P(CTX, None),
        P(CTX),
        P(),
        P(),
    )
    return jax.shard_map(
        shards,
        mesh=torus,
        in_specs=placed,
        out_specs=(P(CTX, HEAD), P(CTX, HEAD), P(ALL, None)),
        check_vma=False,
    )
```

```python
import math

import jax
import jax.numpy as jnp
from jax import lax
from jax.experimental import pallas as pl
from jax.experimental.pallas import tpu as pltpu
from jax.sharding import Mesh
from jax.sharding import PartitionSpec as P

CTX = ("ctx_0", "ctx_1", "ctx_2")
HEAD = ("far", "core")
ALL = CTX + HEAD

LATENT = 576
MAIN_SCALE = 192.0 ** (-0.5)
LOG2E = math.log2(math.e)
bf16, f32 = jnp.bfloat16, jnp.float32


def key_of(place):
    return ((place >> 5) & 31) * 64 + (place >> 10) * 32 + (place & 31)


def lay_halves(keys, own, other, core, width):
    half = own.shape[0]
    keys[pl.ds(pl.multiple_of(core * half, half), half), 0:width] = own[...]
    keys[pl.ds(pl.multiple_of((1 - core) * half, half), half), 0:width] = other[...]


def head_kernel(where, q_hbm, own_hbm, other_hbm, *refs):
    outs, (keys, queries, pair, scores, probs, acc, turned, sems) = refs[:4], refs[4:]
    pairs, rows, both_width = queries.shape
    width = both_width // 2
    half = own_hbm.shape[0]
    n_keys = 2 * half
    wide = keys.shape[1] - rows

    def key_copy(k, source):
        spot = pl.multiple_of((where[0] ^ k) * half, half)
        return pltpu.make_async_copy(
            source.at[:, pl.ds(0, wide)], keys.at[pl.ds(spot, half), pl.ds(0, wide)], sems.at[k]
        )

    def query_copy(p):
        at = pl.multiple_of(p * both_width, 128)
        return pltpu.make_async_copy(
            q_hbm.at[:, pl.ds(at, both_width)], queries.at[p], sems.at[2 + p]
        )

    key_copy(0, own_hbm).start()
    query_copy(0).start()
    key_copy(1, other_hbm).start()
    for p in range(1, pairs):
        query_copy(p).start()
    place = lax.broadcasted_iota(jnp.int32, (n_keys, rows), 0)
    query = lax.broadcasted_iota(jnp.int32, (n_keys, rows), 1)
    keys[:, wide:] = jnp.where(key_of(place) > query + where[1], -1e30, 0.0).astype(bf16)
    pair[:, width:wide] = jnp.zeros((2 * rows, wide - width), bf16)
    row = lax.broadcasted_iota(jnp.int32, (2 * rows, rows), 0)
    lane = lax.broadcasted_iota(jnp.int32, (2 * rows, rows), 1)
    pair[:, wide:] = jnp.where((row & (rows - 1)) == lane, 1.0, 0.0).astype(bf16)
    acc[...] = jnp.zeros(acc.shape, f32)
    scale = MAIN_SCALE * LOG2E
    vec = (8, 2 * rows)
    tall = (n_keys // 8, 8, 2 * rows)
    key_copy(0, own_hbm).wait()
    key_copy(1, other_hbm).wait()

    def add_pair(recip):
        old = (probs[...].astype(f32).reshape(tall) * recip[None]).reshape(n_keys, 2 * rows)
        acc[...] += old[:, :rows] + old[:, rows:]

    def exponentials(shift):
        e = jnp.exp2(scores[...].reshape(tall) * scale - shift[None])
        probs[...] = e.reshape(n_keys, 2 * rows).astype(bf16)
        return jnp.broadcast_to(jnp.sum(jnp.sum(e, axis=0), axis=0, keepdims=True), vec)

    def step(p, carry):
        shift, recip = carry
        query_copy(p).wait()
        both = queries[p]
        pair[0:rows, 0:width] = both[:, :width]
        pair[rows:, 0:width] = both[:, width:]
        add_pair(recip)
        total = exponentials(shift)
        new = lax.dot_general(
            keys[...], pair[...], (((1,), (1,)), ((), ())), preferred_element_type=f32
        )
        scores[...] = new
        top = jnp.max(new.reshape(tall), axis=0)
        top = jnp.broadcast_to(jnp.max(top, axis=0, keepdims=True), vec)
        return top * scale, jnp.where(p > 0, 1.0 / total, 0.0)

    scores[...] = jnp.zeros(scores.shape, f32)
    probs[...] = jnp.zeros(probs.shape, bf16)
    zero = jnp.zeros(vec, f32)
    shift, recip = lax.fori_loop(0, pairs, step, (zero, zero))
    add_pair(recip)
    add_pair(1.0 / exponentials(shift))
    turned[...] = (acc[...] * (1.0 / 128.0)).T.astype(bf16)
    few = rows // 4
    for k in range(4):
        outs[k][...] = turned[pl.ds(pl.multiple_of((where[2] ^ k) * few, few), few), :]


def head_totals(where, q, own, other):
    rows, columns = q.shape
    n_keys = 2 * own.shape[0]
    pairs = columns // (2 * LATENT)
    vmem = pl.BlockSpec(memory_space=pltpu.VMEM)
    anywhere = pl.BlockSpec(memory_space=pl.ANY)
    return pl.pallas_call(
        head_kernel,
        out_shape=[jax.ShapeDtypeStruct((rows // 4, n_keys), bf16)] * 4,
        in_specs=[
            pl.BlockSpec(memory_space=pltpu.SMEM),
            pl.BlockSpec(memory_space=pltpu.HBM),
            anywhere,
            anywhere,
        ],
        out_specs=[vmem] * 4,
        scratch_shapes=[
            pltpu.VMEM((n_keys, 768), bf16),
            pltpu.VMEM((pairs, rows, 2 * LATENT), bf16),
            pltpu.VMEM((2 * rows, 768), bf16),
            pltpu.VMEM((n_keys, 2 * rows), f32),
            pltpu.VMEM((n_keys, 2 * rows), bf16),
            pltpu.VMEM((n_keys, rows), f32),
            pltpu.VMEM((rows, n_keys), bf16),
            pltpu.SemaphoreType.DMA((2 + pairs,)),
        ],
        compiler_params=pltpu.CompilerParams(vmem_limit_bytes=56 * 2**20),
        cost_estimate=pl.CostEstimate(
            flops=2 * 32 * rows * n_keys * 768, bytes_accessed=8 * 2**20, transcendentals=2**23
        ),
        name="head_totals",
    )(where, q, own, other)


IDX_GROUP = 32
IDX_DIM = 128
OWN_HEADS = 16
BIT = [1 << j for j in range(31)] + [-(2**31)]


def forward_kernel(
    where, q_ref, w_ref, own_ref, other_ref, kl_ref, bits_ref, chance_ref, keys, block, logits
):
    g = pl.program_id(0)
    rows, dim = q_ref.shape[0], keys.shape[1]

    @pl.when(g == 0)
    def _():
        lay_halves(keys, own_ref, other_ref, where[0], dim)
        logits[...] = jnp.zeros(logits.shape, f32)

    for j in range(IDX_GROUP):
        block[j * rows : (j + 1) * rows, :] = q_ref[:, j * dim : (j + 1) * dim]
    inner = lax.dot_general(
        block[...], keys[...], (((1,), (1,)), ((), ())), preferred_element_type=f32
    )
    weights = w_ref[0] * (dim ** (-0.5))
    total = logits[...]
    bits = jnp.zeros(total.shape, jnp.int32)
    for j in range(IDX_GROUP):
        part = inner[j * rows : (j + 1) * rows]
        total += jnp.maximum(part, 0.0) * weights[:, j : j + 1]
        bits = bits | jnp.where(part > 0.0, BIT[j], 0)
    logits[...] = total
    bits_ref[...] = bits

    @pl.when(g == pl.num_programs(0) - 1)
    def _():
        place = lax.broadcasted_iota(jnp.int32, logits.shape, 1)
        query = lax.broadcasted_iota(jnp.int32, logits.shape, 0) + where[2] * rows
        seen = key_of(place) <= query + where[1]
        values = jnp.where(seen, total, -1e30)
        e = jnp.where(seen, jnp.exp(values - jnp.max(values, axis=1, keepdims=True)), 0.0)
        chance_ref[...] = e * (kl_ref[...] / jnp.sum(e, axis=1, keepdims=True))


def index_forward(where, q, w, own, other, kl):
    rows, dim = kl.shape[0], IDX_DIM
    n_keys = 2 * own.shape[0]
    heads = q.shape[1] // dim
    wide = IDX_GROUP * dim
    return pl.pallas_call(
        forward_kernel,
        grid_spec=pltpu.PrefetchScalarGridSpec(
            num_scalar_prefetch=1,
            grid=(heads // IDX_GROUP,),
            in_specs=[
                pl.BlockSpec((rows, wide), lambda g, where: (0, g)),
                pl.BlockSpec((1, rows, IDX_GROUP), lambda g, where: (g, 0, 0)),
                pl.BlockSpec((n_keys // 2, dim), lambda g, where: (0, 5)),
                pl.BlockSpec((n_keys // 2, dim), lambda g, where: (0, 5)),
                pl.BlockSpec((rows, 1), lambda g, where: (0, 0)),
            ],
            out_specs=[
                pl.BlockSpec((rows, n_keys), lambda g, where: (g, 0)),
                pl.BlockSpec((rows, n_keys), lambda g, where: (0, 0)),
            ],
            scratch_shapes=[
                pltpu.VMEM((n_keys, dim), bf16),
                pltpu.VMEM((IDX_GROUP * rows, dim), bf16),
                pltpu.VMEM((rows, n_keys), f32),
            ],
        ),
        out_shape=[
            jax.ShapeDtypeStruct((heads // IDX_GROUP * rows, n_keys), jnp.int32),
            jax.ShapeDtypeStruct((rows, n_keys), f32),
        ],
        compiler_params=pltpu.CompilerParams(vmem_limit_bytes=24 * 2**20),
        cost_estimate=pl.CostEstimate(
            flops=2 * heads * rows * n_keys * 256, bytes_accessed=10 * 2**20, transcendentals=2**16
        ),
        name="index_forward",
    )(where, q, w, own, other, kl)


def lay_masked(bits_ref, upstream, masked):
    rows = bits_ref.shape[0]
    bits, up = bits_ref[...], upstream[...].astype(f32)
    for j in range(IDX_GROUP):
        masked[j * rows : (j + 1) * rows, :] = jnp.where(bits & BIT[j] != 0, up, 0.0).astype(bf16)


def query_kernel(where, upstream_ref, bits_ref, q_ref, w_ref, own_ref, other_ref, *refs):
    outs, (keys, masked, grad_ref) = refs[:4], refs[4:]
    g = pl.program_id(0)
    rows, dim = q_ref.shape[0], keys.shape[1]
    wide = grad_ref.shape[2] - 128

    @pl.when(g == 0)
    def _():
        lay_halves(keys, own_ref, other_ref, where[0], dim)

    lay_masked(bits_ref, upstream_ref, masked)
    plain = lax.dot_general(
        masked[...], keys[...], (((1,), (0,)), ((), ())), preferred_element_type=f32
    ) * (dim ** (-0.5))
    lane = lax.broadcasted_iota(jnp.int32, (rows, 128), 1)
    for first in range(0, IDX_GROUP, OWN_HEADS):
        owner = g * (IDX_GROUP // OWN_HEADS) + first // OWN_HEADS
        sums = jnp.zeros((rows, 128), f32)
        for n in range(OWN_HEADS):
            j = first + n
            q = q_ref[:, j * dim : (j + 1) * dim].astype(f32)
            part = plain[j * rows : (j + 1) * rows]
            gain = w_ref[0, :, j : j + 1]
            grad_ref[owner, :, n * dim : (n + 1) * dim] = (part * gain).astype(bf16)
            sums = jnp.where(lane == n, jnp.sum(q * part, axis=1, keepdims=True), sums)
        grad_ref[owner, :, wide:] = sums.astype(bf16)

    @pl.when(g == pl.num_programs(0) - 1)
    def _():
        for k in range(4):
            outs[k][...] = grad_ref[where[2] ^ k]


def key_kernel(where, *refs):
    parts, refs = refs[:4], refs[4:]
    chance_ref, kl_ref, bits_ref, q_ref, w_ref, gk_ref, upstream_ref, masked, block, acc = refs
    g = pl.program_id(0)
    rows, dim = q_ref.shape[0], block.shape[1]

    @pl.when(g == 0)
    def _():
        target = parts[0][...].astype(f32)
        for k in range(1, 4):
            target += parts[k][...].astype(f32)
        upstream_ref[...] = (chance_ref[...] - kl_ref[...] * target).astype(bf16)
        acc[...] = jnp.zeros(acc.shape, f32)

    lay_masked(bits_ref, upstream_ref, masked)
    for j in range(IDX_GROUP):
        q = q_ref[:, j * dim : (j + 1) * dim].astype(f32)
        block[j * rows : (j + 1) * rows, :] = (q * w_ref[0, :, j : j + 1]).astype(bf16)
    acc[...] += lax.dot_general(
        block[...], masked[...], (((0,), (0,)), ((), ())), preferred_element_type=f32
    )

    @pl.when(g == pl.num_programs(0) - 1)
    def _():
        for t in range(acc.shape[1] // 128):
            piece = (acc[:, t * 128 : (t + 1) * 128] * (dim ** (-0.5))).T.astype(bf16)
            for b in range(4):
                place = t * 128 + b * 32
                key = ((place >> 5) & 31) * 64 + (place >> 10) * 32
                gk_ref[key : key + 32, :] = piece[b * 32 : (b + 1) * 32]


def whole(*shape):
    return pl.BlockSpec(shape, lambda g, where: (0,) * len(shape))


def index_query_grads(where, upstream, bits, q, w, own, other):
    rows, n_keys = upstream.shape
    dim = IDX_DIM
    heads = q.shape[1] // dim
    out = jax.ShapeDtypeStruct((rows, heads // 4 * dim + 128), bf16)
    return pl.pallas_call(
        query_kernel,
        grid_spec=pltpu.PrefetchScalarGridSpec(
            num_scalar_prefetch=1,
            grid=(heads // IDX_GROUP,),
            in_specs=[
                whole(rows, n_keys),
                pl.BlockSpec((rows, n_keys), lambda g, where: (g, 0)),
                pl.BlockSpec((rows, IDX_GROUP * dim), lambda g, where: (0, g)),
                pl.BlockSpec((1, rows, IDX_GROUP), lambda g, where: (g, 0, 0)),
                pl.BlockSpec((n_keys // 2, dim), lambda g, where: (0, 5)),
                pl.BlockSpec((n_keys // 2, dim), lambda g, where: (0, 5)),
            ],
            out_specs=[whole(*out.shape)] * 4,
            scratch_shapes=[
                pltpu.VMEM((n_keys, dim), bf16),
                pltpu.VMEM((IDX_GROUP * rows, n_keys), bf16),
                pltpu.VMEM((4, *out.shape), bf16),
            ],
        ),
        out_shape=[out] * 4,
        compiler_params=pltpu.CompilerParams(vmem_limit_bytes=24 * 2**20),
        cost_estimate=pl.CostEstimate(
            flops=4 * heads * rows * n_keys * 128, bytes_accessed=6 * 2**20, transcendentals=0
        ),
        name="index_query_grads",
    )(where, upstream, bits, q, w, own, other)


def index_key_grads(where, parts, chance, kl, bits, q, w):
    rows, n_keys = chance.shape
    dim = IDX_DIM
    heads = q.shape[1] // dim
    return pl.pallas_call(
        key_kernel,
        grid_spec=pltpu.PrefetchScalarGridSpec(
            num_scalar_prefetch=1,
            grid=(heads // IDX_GROUP,),
            in_specs=[
                *[whole(rows, n_keys)] * 5,
                whole(rows, 1),
                pl.BlockSpec((rows, n_keys), lambda g, where: (g, 0)),
                pl.BlockSpec((rows, IDX_GROUP * dim), lambda g, where: (0, g)),
                pl.BlockSpec((1, rows, IDX_GROUP), lambda g, where: (g, 0, 0)),
            ],
            out_specs=[whole(n_keys, dim), whole(rows, n_keys)],
            scratch_shapes=[
                pltpu.VMEM((IDX_GROUP * rows, n_keys), bf16),
                pltpu.VMEM((IDX_GROUP * rows, dim), bf16),
                pltpu.VMEM((dim, n_keys), f32),
            ],
        ),
        out_shape=[
            jax.ShapeDtypeStruct((n_keys, dim), bf16),
            jax.ShapeDtypeStruct((rows, n_keys), bf16),
        ],
        compiler_params=pltpu.CompilerParams(vmem_limit_bytes=24 * 2**20),
        cost_estimate=pl.CostEstimate(
            flops=4 * heads * rows * n_keys * 128, bytes_accessed=6 * 2**20, transcendentals=0
        ),
        name="index_key_grads",
    )(where, *parts, chance, kl, bits, q, w)


def to_all(piece, axes):
    copies = jnp.broadcast_to(piece, (lax.axis_size(axes), *piece.shape))
    return lax.all_to_all(copies, axes, split_axis=0, concat_axis=0, tiled=True)


def finish_kernel(where, *refs):
    grads, (key_ref, query_out, weight_out, key_out, wide_weight) = refs[:4], refs[4:]
    few, wide = grads[0].shape[0], query_out.shape[1]
    for k in range(4):
        at = pl.ds(pl.multiple_of((where[2] ^ k) * few, few), few)
        query_out[at, :] = grads[k][:, :wide].astype(f32)
        wide_weight[at, :] = grads[k][:, wide:].astype(f32)
    weight_out[...] = wide_weight[...].T[: weight_out.shape[0]]
    key_out[...] = jnp.sum(key_ref[...].astype(f32), axis=0)


def finish(where, grads, keys):
    rows = 4 * grads[0].shape[0]
    vmem = pl.BlockSpec(memory_space=pltpu.VMEM)
    return pl.pallas_call(
        finish_kernel,
        out_shape=[
            jax.ShapeDtypeStruct((rows, OWN_HEADS * IDX_DIM), f32),
            jax.ShapeDtypeStruct((OWN_HEADS, rows), f32),
            jax.ShapeDtypeStruct(keys.shape[1:], f32),
        ],
        in_specs=[pl.BlockSpec(memory_space=pltpu.SMEM)] + [vmem] * 5,
        out_specs=[vmem] * 3,
        scratch_shapes=[pltpu.VMEM((rows, 128), f32)],
        compiler_params=pltpu.CompilerParams(vmem_limit_bytes=16 * 2**20),
        cost_estimate=pl.CostEstimate(flops=2**20, bytes_accessed=2**21, transcendentals=0),
        name="finish",
    )(where, *grads, keys)


def swap_heads(pieces):
    count = len(pieces)
    return [pieces[0]] + [
        lax.ppermute(pieces[k], HEAD, [(h, h ^ k) for h in range(count)]) for k in range(1, count)
    ]


def shards(
    main_query, latents, idx_query, idx_weight, idx_keys, kl_cotangent, query_start, key_start
):
    rows = main_query.shape[0]
    core = lax.axis_index("core")
    head = lax.axis_index(HEAD)
    few = rows // lax.axis_size(HEAD)
    offset = query_start[0] + lax.axis_index(CTX) * rows - key_start[0]
    where = jnp.stack([core, offset, head]).astype(jnp.int32)

    half = latents.shape[0] // 2
    slab = jnp.concatenate([jnp.pad(latents, ((0, 0), (0, 64))), idx_keys], axis=1)
    own = to_all(lax.dynamic_slice_in_dim(slab, core * half, half, 0), CTX)
    own = own.reshape(-1, own.shape[-1])
    other = lax.ppermute(own, "core", [(0, 1), (1, 0)])

    kl = lax.dynamic_slice_in_dim(kl_cotangent, head * few, few, 0)[:, None]
    w = lax.dynamic_slice_in_dim(idx_weight, head * few, few, 0)
    w = w.reshape(few, -1, IDX_GROUP).transpose(1, 0, 2)

    few_queries = lax.dynamic_slice_in_dim(idx_query, head * few, few, 0)

    parts = swap_heads(head_totals(where, main_query, own, other))
    bits, chance = index_forward(where, few_queries, w, own, other, kl)
    gk, upstream = index_key_grads(where, parts, chance, kl, bits, few_queries, w)
    pieces = lax.all_to_all(gk.reshape(lax.axis_size(ALL), -1, gk.shape[1]), ALL, 0, 0, tiled=True)
    grads = index_query_grads(where, upstream, bits, few_queries, w, own, other)
    grad_query, grad_weight, grad_keys = finish(where, swap_heads(grads), pieces)
    return grad_query, grad_weight.T, grad_keys


def solution(mesh):
    torus = Mesh(mesh.devices.reshape(2, 4, 4, 2, 2), ALL)
    placed = (
        P(CTX, HEAD),
        P(CTX, None),
        P(CTX, None),
        P(CTX, None),
        P(CTX, None),
        P(CTX),
        P(),
        P(),
    )
    return jax.shard_map(
        shards,
        mesh=torus,
        in_specs=placed,
        out_specs=(P(CTX, HEAD), P(CTX, HEAD), P(ALL, None)),
        check_vma=False,
    )
```

```python
import math

import jax
import jax.numpy as jnp
from jax import lax
from jax.experimental import pallas as pl
from jax.experimental.pallas import tpu as pltpu
from jax.sharding import Mesh
from jax.sharding import PartitionSpec as P

CTX = ("ctx_0", "ctx_1", "ctx_2")
HEAD = ("far", "core")
ALL = CTX + HEAD

LATENT = 576
MAIN_SCALE = 192.0 ** (-0.5)
LOG2E = math.log2(math.e)
bf16, f32 = jnp.bfloat16, jnp.float32


def key_of(place):
    return ((place >> 5) & 31) * 64 + (place >> 10) * 32 + (place & 31)


def lay_halves(keys, own, other, core, width):
    half = own.shape[0]
    keys[pl.ds(pl.multiple_of(core * half, half), half), 0:width] = own[...]
    keys[pl.ds(pl.multiple_of((1 - core) * half, half), half), 0:width] = other[...]


def head_kernel(where, q_hbm, own_hbm, other_hbm, *refs):
    outs, (keys, queries, pair, scores, probs, acc, turned, sems) = refs[:4], refs[4:]
    pairs, rows, both_width = queries.shape
    width = both_width // 2
    half = own_hbm.shape[0]
    n_keys = 2 * half
    wide = keys.shape[1] - rows

    def key_copy(k, source):
        spot = pl.multiple_of((where[0] ^ k) * half, half)
        return pltpu.make_async_copy(
            source.at[:, pl.ds(0, wide)], keys.at[pl.ds(spot, half), pl.ds(0, wide)], sems.at[k]
        )

    def query_copy(p):
        at = pl.multiple_of(p * both_width, 128)
        return pltpu.make_async_copy(
            q_hbm.at[:, pl.ds(at, both_width)], queries.at[p], sems.at[2 + p]
        )

    key_copy(0, own_hbm).start()
    query_copy(0).start()
    key_copy(1, other_hbm).start()
    for p in range(1, pairs):
        query_copy(p).start()
    place = lax.broadcasted_iota(jnp.int32, (n_keys, rows), 0)
    query = lax.broadcasted_iota(jnp.int32, (n_keys, rows), 1)
    keys[:, wide:] = jnp.where(key_of(place) > query + where[1], -1e30, 0.0).astype(bf16)
    pair[:, width:wide] = jnp.zeros((2 * rows, wide - width), bf16)
    row = lax.broadcasted_iota(jnp.int32, (2 * rows, rows), 0)
    lane = lax.broadcasted_iota(jnp.int32, (2 * rows, rows), 1)
    pair[:, wide:] = jnp.where((row & (rows - 1)) == lane, 1.0, 0.0).astype(bf16)
    acc[...] = jnp.zeros(acc.shape, f32)
    scale = MAIN_SCALE * LOG2E
    vec = (8, 2 * rows)
    tall = (n_keys // 8, 8, 2 * rows)
    key_copy(0, own_hbm).wait()
    key_copy(1, other_hbm).wait()

    def add_pair(recip):
        old = (probs[...].astype(f32).reshape(tall) * recip[None]).reshape(n_keys, 2 * rows)
        acc[...] += old[:, :rows] + old[:, rows:]

    def exponentials(shift):
        e = jnp.exp2(scores[...].reshape(tall) * scale - shift[None])
        probs[...] = e.reshape(n_keys, 2 * rows).astype(bf16)
        return jnp.broadcast_to(jnp.sum(jnp.sum(e, axis=0), axis=0, keepdims=True), vec)

    def step(p, carry):
        shift, recip = carry
        query_copy(p).wait()
        both = queries[p]
        pair[0:rows, 0:width] = both[:, :width]
        pair[rows:, 0:width] = both[:, width:]
        add_pair(recip)
        total = exponentials(shift)
        new = lax.dot_general(
            keys[...], pair[...], (((1,), (1,)), ((), ())), preferred_element_type=f32
        )
        scores[...] = new
        top = jnp.max(new.reshape(tall), axis=0)
        top = jnp.broadcast_to(jnp.max(top, axis=0, keepdims=True), vec)
        return top * scale, jnp.where(p > 0, 1.0 / total, 0.0)

    scores[...] = jnp.zeros(scores.shape, f32)
    probs[...] = jnp.zeros(probs.shape, bf16)
    zero = jnp.zeros(vec, f32)
    shift, recip = lax.fori_loop(0, pairs, step, (zero, zero))
    add_pair(recip)
    add_pair(1.0 / exponentials(shift))
    turned[...] = (acc[...] * (1.0 / 128.0)).T.astype(bf16)
    few = rows // 4
    for k in range(4):
        outs[k][...] = turned[pl.ds(pl.multiple_of((where[2] ^ k) * few, few), few), :]


def head_totals(where, q, own, other):
    rows, columns = q.shape
    n_keys = 2 * own.shape[0]
    pairs = columns // (2 * LATENT)
    vmem = pl.BlockSpec(memory_space=pltpu.VMEM)
    anywhere = pl.BlockSpec(memory_space=pl.ANY)
    return pl.pallas_call(
        head_kernel,
        out_shape=[jax.ShapeDtypeStruct((rows // 4, n_keys), bf16)] * 4,
        in_specs=[
            pl.BlockSpec(memory_space=pltpu.SMEM),
            pl.BlockSpec(memory_space=pltpu.HBM),
            anywhere,
            anywhere,
        ],
        out_specs=[vmem] * 4,
        scratch_shapes=[
            pltpu.VMEM((n_keys, 768), bf16),
            pltpu.VMEM((pairs, rows, 2 * LATENT), bf16),
            pltpu.VMEM((2 * rows, 768), bf16),
            pltpu.VMEM((n_keys, 2 * rows), f32),
            pltpu.VMEM((n_keys, 2 * rows), bf16),
            pltpu.VMEM((n_keys, rows), f32),
            pltpu.VMEM((rows, n_keys), bf16),
            pltpu.SemaphoreType.DMA((2 + pairs,)),
        ],
        compiler_params=pltpu.CompilerParams(vmem_limit_bytes=56 * 2**20),
        cost_estimate=pl.CostEstimate(
            flops=2 * 32 * rows * n_keys * 768, bytes_accessed=8 * 2**20, transcendentals=2**23
        ),
        name="head_totals",
    )(where, q, own, other)


IDX_GROUP = 32
IDX_DIM = 128
OWN_HEADS = 16
BIT = [1 << j for j in range(31)] + [-(2**31)]


def forward_kernel(where, q_ref, w_ref, own_ref, other_ref, kl_ref, *refs):
    bits_ref, chance_ref, gained_ref, keys, block, gained, logits = refs
    g = pl.program_id(0)
    rows, dim = q_ref.shape[0], keys.shape[1]

    @pl.when(g == 0)
    def _():
        lay_halves(keys, own_ref, other_ref, where[0], dim)
        logits[...] = jnp.zeros(logits.shape, f32)

    for j in range(IDX_GROUP):
        at = slice(j * rows, (j + 1) * rows)
        block[at, :] = q_ref[:, j * dim : (j + 1) * dim]
        gained[at, :] = q_ref[:, j * dim : (j + 1) * dim].astype(f32) * w_ref[0, :, j : j + 1]
    gained_ref[...] = gained[...].T.astype(bf16)
    inner = lax.dot_general(
        block[...], keys[...], (((1,), (1,)), ((), ())), preferred_element_type=f32
    )
    weights = w_ref[0] * (dim ** (-0.5))
    total = logits[...]
    bits = jnp.zeros(total.shape, jnp.int32)
    for j in range(IDX_GROUP):
        part = inner[j * rows : (j + 1) * rows]
        total += jnp.maximum(part, 0.0) * weights[:, j : j + 1]
        bits = bits | jnp.where(part > 0.0, BIT[j], 0)
    logits[...] = total
    bits_ref[...] = bits

    @pl.when(g == pl.num_programs(0) - 1)
    def _():
        place = lax.broadcasted_iota(jnp.int32, logits.shape, 1)
        query = lax.broadcasted_iota(jnp.int32, logits.shape, 0) + where[2] * rows
        seen = key_of(place) <= query + where[1]
        values = jnp.where(seen, total, -1e30)
        e = jnp.where(seen, jnp.exp(values - jnp.max(values, axis=1, keepdims=True)), 0.0)
        chance_ref[...] = e * (kl_ref[...] / jnp.sum(e, axis=1, keepdims=True))


def index_forward(where, q, w, own, other, kl):
    rows, dim = kl.shape[0], IDX_DIM
    n_keys = 2 * own.shape[0]
    heads = q.shape[1] // dim
    wide = IDX_GROUP * dim
    return pl.pallas_call(
        forward_kernel,
        grid_spec=pltpu.PrefetchScalarGridSpec(
            num_scalar_prefetch=1,
            grid=(heads // IDX_GROUP,),
            in_specs=[
                pl.BlockSpec((rows, wide), lambda g, where: (0, g)),
                pl.BlockSpec((1, rows, IDX_GROUP), lambda g, where: (g, 0, 0)),
                pl.BlockSpec((n_keys // 2, dim), lambda g, where: (0, 5)),
                pl.BlockSpec((n_keys // 2, dim), lambda g, where: (0, 5)),
                pl.BlockSpec((rows, 1), lambda g, where: (0, 0)),
            ],
            out_specs=[
                pl.BlockSpec((rows, n_keys), lambda g, where: (g, 0)),
                pl.BlockSpec((rows, n_keys), lambda g, where: (0, 0)),
                pl.BlockSpec((dim, IDX_GROUP * rows), lambda g, where: (0, g)),
            ],
            scratch_shapes=[
                pltpu.VMEM((n_keys, dim), bf16),
                pltpu.VMEM((IDX_GROUP * rows, dim), bf16),
                pltpu.VMEM((IDX_GROUP * rows, dim), f32),
                pltpu.VMEM((rows, n_keys), f32),
            ],
        ),
        out_shape=[
            jax.ShapeDtypeStruct((heads // IDX_GROUP * rows, n_keys), jnp.int32),
            jax.ShapeDtypeStruct((rows, n_keys), f32),
            jax.ShapeDtypeStruct((dim, heads * rows), bf16),
        ],
        compiler_params=pltpu.CompilerParams(vmem_limit_bytes=24 * 2**20),
        cost_estimate=pl.CostEstimate(
            flops=2 * heads * rows * n_keys * 256, bytes_accessed=10 * 2**20, transcendentals=2**16
        ),
        name="index_forward",
    )(where, q, w, own, other, kl)


def lay_masked(bits_ref, upstream, masked):
    rows = bits_ref.shape[0]
    bits, up = bits_ref[...], upstream[...].astype(f32)
    for j in range(IDX_GROUP):
        masked[j * rows : (j + 1) * rows, :] = jnp.where(bits & BIT[j] != 0, up, 0.0).astype(bf16)


def query_kernel(where, upstream_ref, bits_ref, q_ref, w_ref, own_ref, other_ref, *refs):
    outs, (keys, masked, grad_ref) = refs[:4], refs[4:]
    g = pl.program_id(0)
    rows, dim = q_ref.shape[0], keys.shape[1]
    wide = grad_ref.shape[2] - 128

    @pl.when(g == 0)
    def _():
        lay_halves(keys, own_ref, other_ref, where[0], dim)

    lay_masked(bits_ref, upstream_ref, masked)
    plain = lax.dot_general(
        masked[...], keys[...], (((1,), (0,)), ((), ())), preferred_element_type=f32
    ) * (dim ** (-0.5))
    lane = lax.broadcasted_iota(jnp.int32, (rows, 128), 1)
    for first in range(0, IDX_GROUP, OWN_HEADS):
        owner = g * (IDX_GROUP // OWN_HEADS) + first // OWN_HEADS
        sums = jnp.zeros((rows, 128), f32)
        for n in range(OWN_HEADS):
            j = first + n
            q = q_ref[:, j * dim : (j + 1) * dim].astype(f32)
            part = plain[j * rows : (j + 1) * rows]
            gain = w_ref[0, :, j : j + 1]
            grad_ref[owner, :, n * dim : (n + 1) * dim] = (part * gain).astype(bf16)
            sums = jnp.where(lane == n, jnp.sum(q * part, axis=1, keepdims=True), sums)
        grad_ref[owner, :, wide:] = sums.astype(bf16)

    @pl.when(g == pl.num_programs(0) - 1)
    def _():
        for k in range(4):
            outs[k][...] = grad_ref[where[2] ^ k]


def key_kernel(where, *refs):
    parts, refs = refs[:4], refs[4:]
    chance_ref, kl_ref, bits_ref, gained_ref, gk_ref, upstream_ref, masked, acc = refs
    g = pl.program_id(0)
    dim = acc.shape[0]

    @pl.when(g == 0)
    def _():
        target = parts[0][...].astype(f32)
        for k in range(1, 4):
            target += parts[k][...].astype(f32)
        upstream_ref[...] = (chance_ref[...] - kl_ref[...] * target).astype(bf16)
        acc[...] = jnp.zeros(acc.shape, f32)

    lay_masked(bits_ref, upstream_ref, masked)
    acc[...] += lax.dot_general(
        gained_ref[...], masked[...], (((1,), (0,)), ((), ())), preferred_element_type=f32
    )

    @pl.when(g == pl.num_programs(0) - 1)
    def _():
        for t in range(acc.shape[1] // 128):
            piece = (acc[:, t * 128 : (t + 1) * 128] * (dim ** (-0.5))).T.astype(bf16)
            for b in range(4):
                place = t * 128 + b * 32
                key = ((place >> 5) & 31) * 64 + (place >> 10) * 32
                gk_ref[key : key + 32, :] = piece[b * 32 : (b + 1) * 32]


def whole(*shape):
    return pl.BlockSpec(shape, lambda g, where: (0,) * len(shape))


def index_query_grads(where, upstream, bits, q, w, own, other):
    rows, n_keys = upstream.shape
    dim = IDX_DIM
    heads = q.shape[1] // dim
    out = jax.ShapeDtypeStruct((rows, heads // 4 * dim + 128), bf16)
    return pl.pallas_call(
        query_kernel,
        grid_spec=pltpu.PrefetchScalarGridSpec(
            num_scalar_prefetch=1,
            grid=(heads // IDX_GROUP,),
            in_specs=[
                whole(rows, n_keys),
                pl.BlockSpec((rows, n_keys), lambda g, where: (g, 0)),
                pl.BlockSpec((rows, IDX_GROUP * dim), lambda g, where: (0, g)),
                pl.BlockSpec((1, rows, IDX_GROUP), lambda g, where: (g, 0, 0)),
                pl.BlockSpec((n_keys // 2, dim), lambda g, where: (0, 5)),
                pl.BlockSpec((n_keys // 2, dim), lambda g, where: (0, 5)),
            ],
            out_specs=[whole(*out.shape)] * 4,
            scratch_shapes=[
                pltpu.VMEM((n_keys, dim), bf16),
                pltpu.VMEM((IDX_GROUP * rows, n_keys), bf16),
                pltpu.VMEM((4, *out.shape), bf16),
            ],
        ),
        out_shape=[out] * 4,
        compiler_params=pltpu.CompilerParams(vmem_limit_bytes=24 * 2**20),
        cost_estimate=pl.CostEstimate(
            flops=4 * heads * rows * n_keys * 128, bytes_accessed=6 * 2**20, transcendentals=0
        ),
        name="index_query_grads",
    )(where, upstream, bits, q, w, own, other)


def index_key_grads(where, parts, chance, kl, bits, gained):
    rows, n_keys = chance.shape
    dim = IDX_DIM
    heads = gained.shape[1] // rows
    return pl.pallas_call(
        key_kernel,
        grid_spec=pltpu.PrefetchScalarGridSpec(
            num_scalar_prefetch=1,
            grid=(heads // IDX_GROUP,),
            in_specs=[
                *[whole(rows, n_keys)] * 5,
                whole(rows, 1),
                pl.BlockSpec((rows, n_keys), lambda g, where: (g, 0)),
                pl.BlockSpec((dim, IDX_GROUP * rows), lambda g, where: (0, g)),
            ],
            out_specs=[whole(n_keys, dim), whole(rows, n_keys)],
            scratch_shapes=[
                pltpu.VMEM((IDX_GROUP * rows, n_keys), bf16),
                pltpu.VMEM((dim, n_keys), f32),
            ],
        ),
        out_shape=[
            jax.ShapeDtypeStruct((n_keys, dim), bf16),
            jax.ShapeDtypeStruct((rows, n_keys), bf16),
        ],
        compiler_params=pltpu.CompilerParams(vmem_limit_bytes=24 * 2**20),
        cost_estimate=pl.CostEstimate(
            flops=4 * heads * rows * n_keys * 128, bytes_accessed=6 * 2**20, transcendentals=0
        ),
        name="index_key_grads",
    )(where, *parts, chance, kl, bits, gained)


def to_all(piece, axes):
    copies = jnp.broadcast_to(piece, (lax.axis_size(axes), *piece.shape))
    return lax.all_to_all(copies, axes, split_axis=0, concat_axis=0, tiled=True)


def finish_kernel(where, *refs):
    grads, (key_ref, query_out, weight_out, key_out, wide_weight) = refs[:4], refs[4:]
    few, wide = grads[0].shape[0], query_out.shape[1]
    for k in range(4):
        at = pl.ds(pl.multiple_of((where[2] ^ k) * few, few), few)
        query_out[at, :] = grads[k][:, :wide].astype(f32)
        wide_weight[at, :] = grads[k][:, wide:].astype(f32)
    weight_out[...] = wide_weight[...].T[: weight_out.shape[0]]
    key_out[...] = jnp.sum(key_ref[...].astype(f32), axis=0)


def finish(where, grads, keys):
    rows = 4 * grads[0].shape[0]
    vmem = pl.BlockSpec(memory_space=pltpu.VMEM)
    return pl.pallas_call(
        finish_kernel,
        out_shape=[
            jax.ShapeDtypeStruct((rows, OWN_HEADS * IDX_DIM), f32),
            jax.ShapeDtypeStruct((OWN_HEADS, rows), f32),
            jax.ShapeDtypeStruct(keys.shape[1:], f32),
        ],
        in_specs=[pl.BlockSpec(memory_space=pltpu.SMEM)] + [vmem] * 5,
        out_specs=[vmem] * 3,
        scratch_shapes=[pltpu.VMEM((rows, 128), f32)],
        compiler_params=pltpu.CompilerParams(vmem_limit_bytes=16 * 2**20),
        cost_estimate=pl.CostEstimate(flops=2**20, bytes_accessed=2**21, transcendentals=0),
        name="finish",
    )(where, *grads, keys)


def swap_heads(pieces):
    count = len(pieces)
    return [pieces[0]] + [
        lax.ppermute(pieces[k], HEAD, [(h, h ^ k) for h in range(count)]) for k in range(1, count)
    ]


def shards(
    main_query, latents, idx_query, idx_weight, idx_keys, kl_cotangent, query_start, key_start
):
    rows = main_query.shape[0]
    core = lax.axis_index("core")
    head = lax.axis_index(HEAD)
    few = rows // lax.axis_size(HEAD)
    offset = query_start[0] + lax.axis_index(CTX) * rows - key_start[0]
    where = jnp.stack([core, offset, head]).astype(jnp.int32)

    half = latents.shape[0] // 2
    slab = jnp.concatenate([jnp.pad(latents, ((0, 0), (0, 64))), idx_keys], axis=1)
    own = to_all(lax.dynamic_slice_in_dim(slab, core * half, half, 0), CTX)
    own = own.reshape(-1, own.shape[-1])
    other = lax.ppermute(own, "core", [(0, 1), (1, 0)])

    kl = lax.dynamic_slice_in_dim(kl_cotangent, head * few, few, 0)[:, None]
    w = lax.dynamic_slice_in_dim(idx_weight, head * few, few, 0)
    w = w.reshape(few, -1, IDX_GROUP).transpose(1, 0, 2)

    few_queries = lax.dynamic_slice_in_dim(idx_query, head * few, few, 0)

    parts = swap_heads(head_totals(where, main_query, own, other))
    bits, chance, gained = index_forward(where, few_queries, w, own, other, kl)
    gk, upstream = index_key_grads(where, parts, chance, kl, bits, gained)
    pieces = lax.all_to_all(gk.reshape(lax.axis_size(ALL), -1, gk.shape[1]), ALL, 0, 0, tiled=True)
    grads = index_query_grads(where, upstream, bits, few_queries, w, own, other)
    grad_query, grad_weight, grad_keys = finish(where, swap_heads(grads), pieces)
    return grad_query, grad_weight.T, grad_keys


def solution(mesh):
    torus = Mesh(mesh.devices.reshape(2, 4, 4, 2, 2), ALL)
    placed = (
        P(CTX, HEAD),
        P(CTX, None),
        P(CTX, None),
        P(CTX, None),
        P(CTX, None),
        P(CTX),
        P(),
        P(),
    )
    return jax.shard_map(
        shards,
        mesh=torus,
        in_specs=placed,
        out_specs=(P(CTX, HEAD), P(CTX, HEAD), P(ALL, None)),
        check_vma=False,
    )
```
